32 devices in a mesh: seq: 16 (over z, y, x), tp: 2 (over core).
Axes of the slice: x: 2, y: 2, z: 4, core: 2. Of those that a mesh axis runs over, the one named last changes fastest.
Arguments:
- slab: bfloat16 [6144, 5120], P('seq', 'tp'), may hold values from -6 to 6
- token_request: int32 [6144, 1], P('seq'), may hold values from 0 to 31; in each aligned block of 384 rows (0 to 383, 384 to 767, ...) at most 24 rows name the same one
- request_slot: int32 [32], replicated, may hold values from 0 to 31, each once
- new_states: bfloat16 [32, 3, 5120], P('seq', None, 'tp'), may hold values from -6 to 6
- cache_gain: float32 [5120], replicated, may hold values from 0.25 to 1.75
- query_gain: float32 [5120], replicated, may hold values from 0.25 to 1.75
- key_weight: bfloat16 [5120, 3072], P('seq', 'tp'), may hold values from -0.078125 to 0.078125
- value_weight: bfloat16 [5120, 3072], P('seq', 'tp'), may hold values from -0.078125 to 0.078125
- query_weight: bfloat16 [5120, 3072], P('seq', 'tp'), may hold values from -0.078125 to 0.078125
Outputs:
- attended: bfloat16 [32, 3, 3072], P('seq', None, 'tp')
The draws below stay inside these ranges and needn't reach their ends.
Inputs may be any that keep to these rules, and one draw needn't show every extreme that they name: `token_request`: in each aligned block of 384 tokens no request is named more than 24 times. `request_slot`: each slot is named by exactly one request.
All inputs are finite; a program needn't handle non-finite values.
Results may differ from the reference program's by a relative error of at most 0.0084.
Values may be sent and summed in bfloat16 or wider, within the bound.
No kernel may reach another device: no remote copies, remote signals or barrier semaphores. Data moves between devices by JAX's collectives and lax.ppermute only.
A program may use at most 128 MiB of HBM per device.

```python
import math
import jax
import jax.numpy as jnp
import numpy as np
from jax import lax

D = 5120
HEAD = 128
HEADS = 24
TOK_DEV = 384
STEPS = 3
TOKENS = 6144
REQUESTS = 32
CAP = 24


def block_levels(stream_key, extent, split, smallest, top_value):
    gain, own = 1.0, jax.random.fold_in(stream_key, 6)
    for position, blocks in split:
        draws = jnp.exp(jax.random.uniform(jax.random.fold_in(own, position), (blocks,), jnp.float32, smallest / len(split), top_value / len(split)))
        gain = gain * jnp.repeat(draws, extent[position] // blocks).reshape([-1 if axis == position else 1 for axis in range(len(extent))])
    return gain


def shared_out(rng, own, number, rows, number_of, top, most, lean):
    sequence = jax.random.permutation(rng, number_of)
    heavy_load, common = shares(number_of, rows * top, most, lean, True), shares(number_of, rows * top, most, lean, False)
    places = jnp.arange(number_of)

    def named(tallies, offset_by):
        used = int((tallies > 0).sum())
        fixed = max(1, used // 4)
        passed = fixed + (places - fixed + offset_by * (used - fixed)) % max(1, number_of - fixed)
        return jnp.zeros((number_of,), jnp.int32).at[sequence[jnp.where(places < fixed, places, passed)]].set(jnp.asarray(tallies, jnp.int32))

    tallies = jnp.where(number % 4 == 0, named(heavy_load, number // 4), named(common, number - number // 4 - 1))
    mixed = jax.random.permutation(jax.random.fold_in(own, 3), number_of)
    source_of, taker = mixed[0:number_of // 2 * 2:2], mixed[1:number_of // 2 * 2:2]
    margin = jnp.minimum(tallies[source_of] - 1, most - tallies[taker]) // 2
    margin = jnp.where((source_of == sequence[0]) | (taker == sequence[0]) | (tallies[taker] == 0), 0, jnp.maximum(margin, 0))
    passed = jax.random.randint(jax.random.fold_in(own, 4), (number_of // 2,), 0, 1 << 20) % (margin + 1)
    tallies = tallies.at[source_of].add(-passed).at[taker].add(passed)
    members = jnp.searchsorted(jnp.cumsum(tallies), jnp.arange(rows * top), side="right").astype(jnp.int32)
    grid = members.reshape(top, rows).T
    grid = grid[jax.random.permutation(jax.random.fold_in(own, 1), rows)]
    offset_by = jax.random.randint(jax.random.fold_in(own, 2), (rows, 1), 0, top)
    return jnp.take_along_axis(grid, (jnp.arange(top)[None, :] + offset_by) % top, axis=1)


def shares(amount, total, limit, slope, full):
    loads = [(1 << 20) // math.isqrt(grade ** slope) + 1 for grade in range(1, amount + 1)]
    largest = limit if full else min(limit, max(-(-total // amount), total * loads[0] // sum(loads)))
    least = 1 if total - largest >= amount - 1 else 0
    counts, surplus = [largest] + [least] * (amount - 1), total - largest - least * (amount - 1)
    while surplus > 0:
        movable = [i for i in range(1, amount) if counts[i] < largest] or [i for i in range(1, amount) if counts[i] < limit]
        whole, left = sum([loads[i] for i in movable]), surplus
        for i in movable:
            more = min(limit - counts[i], max(1, left * loads[i] // whole), surplus)
            counts[i] = counts[i] + more
            surplus = surplus - more
    return np.array(counts)


def normal_values(rng, extent, spread, most, split=(), held_as=jnp.bfloat16):
    level = block_levels(rng, extent, split, -0.22, 0.18) if split else 1.0
    drawn = jax.random.normal(rng, extent, jnp.float32) * spread * level
    return jnp.minimum(jnp.maximum(drawn, -most), most).astype(held_as)


def setup_inputs(seed: int = 0) -> dict:
    splits = jax.random.split(jax.random.key(seed), 10)
    slab = normal_values(splits[0], (TOKENS, D), 1.0, 6.0, ((0, 16), (1, 2)))
    token_request_keys = jax.random.split(jax.random.fold_in(splits[1], 1), TOKENS // TOK_DEV)
    token_request_turns = jax.random.permutation(jax.random.fold_in(splits[1], 3), TOKENS // TOK_DEV)
    token_request = jax.vmap(lambda own, number: shared_out(jax.random.fold_in(splits[1], 2), own, number, TOK_DEV, REQUESTS, 1, CAP, 2))(token_request_keys, token_request_turns).reshape((TOKENS, 1))
    request_slot = jax.random.permutation(splits[2], REQUESTS).astype(jnp.int32)
    new_states = normal_values(splits[3], (REQUESTS, STEPS, D), 1.0, 6.0, ((0, 16), (2, 2)))
    cache_gain = jnp.clip(1.0 + 0.15 * jax.random.normal(splits[4], (D,), jnp.float32), 0.25, 1.75)
    query_gain = jnp.clip(1.0 + 0.15 * jax.random.normal(splits[5], (D,), jnp.float32), 0.25, 1.75)
    key_weight = normal_values(splits[6], (D, HEADS * HEAD), D ** -0.5, 0.078125, ((0, 16), (1, 2)))
    value_weight = normal_values(splits[7], (D, HEADS * HEAD), D ** -0.5, 0.078125, ((0, 16), (1, 2)))
    query_weight = normal_values(splits[8], (D, HEADS * HEAD), D ** -0.5, 0.078125, ((0, 16), (1, 2)))
    return {"slab": slab, "token_request": token_request, "request_slot": request_slot, "new_states": new_states, "cache_gain": cache_gain, "query_gain": query_gain, "key_weight": key_weight, "value_weight": value_weight, "query_weight": query_weight}


def scale_rows(hidden_rows, norm_gain):
    values = hidden_rows.astype(jnp.float32)
    factor = lax.rsqrt(lax.optimization_barrier(jnp.mean(values * values, axis=-1, keepdims=True)) + 1e-06)
    return (values * factor * norm_gain).astype(jnp.bfloat16)

def reference(slab, token_request, request_slot, new_states, cache_gain, query_gain, key_weight, value_weight, query_weight):
    normed_slab = scale_rows(slab, cache_gain)
    slab_keys = jnp.dot(normed_slab, key_weight, preferred_element_type=jnp.float32).astype(jnp.bfloat16)
    slab_values = jnp.dot(normed_slab, value_weight, preferred_element_type=jnp.float32).astype(jnp.bfloat16)
    slot_count, step_count, model_width = new_states.shape
    normed_state = scale_rows(new_states, cache_gain).reshape(slot_count * step_count, model_width)
    normed_query = scale_rows(new_states, query_gain).reshape(slot_count * step_count, model_width)
    state_keys = jnp.dot(normed_state, key_weight, preferred_element_type=jnp.float32).astype(jnp.bfloat16)
    state_values = jnp.dot(normed_state, value_weight, preferred_element_type=jnp.float32).astype(jnp.bfloat16)
    queries = jnp.dot(normed_query, query_weight, preferred_element_type=jnp.float32).astype(jnp.bfloat16)
    state_keys = state_keys.reshape(slot_count, step_count, HEADS, HEAD)
    state_values = state_values.reshape(slot_count, step_count, HEADS, HEAD)
    queries = queries.reshape(slot_count, step_count, HEADS, HEAD)
    token_slot = request_slot[token_request[:, 0]]
    cache_keys = slab_keys.astype(jnp.float32).reshape(-1, HEADS, HEAD)
    cache_values = slab_values.astype(jnp.float32).reshape(-1, HEADS, HEAD)
    step_ids = jnp.arange(step_count, dtype=jnp.int32)
    causal = (step_ids[None, :] <= step_ids[:, None]).astype(jnp.float32)
    score_scale = 1.0 / math.sqrt(HEAD)

    def slot_output(slot_index):
        query_block = lax.dynamic_index_in_dim(queries, slot_index, 0, keepdims=False).astype(jnp.float32)
        own_keys = lax.dynamic_index_in_dim(state_keys, slot_index, 0, keepdims=False).astype(jnp.float32)
        own_values = lax.dynamic_index_in_dim(state_values, slot_index, 0, keepdims=False).astype(jnp.float32)
        present = (token_slot == slot_index).astype(jnp.float32)
        scores = jnp.einsum('she,khe->shk', query_block, cache_keys) * score_scale
        weights = jnp.exp(scores) * present[None, None, :]
        own_scores = jnp.einsum('she,the->sht', query_block, own_keys) * score_scale
        own_weights = jnp.exp(own_scores) * causal[:, None, :]
        denominator = lax.optimization_barrier(jnp.sum(weights, axis=-1)) + lax.optimization_barrier(jnp.sum(own_weights, axis=-1))
        probs = lax.optimization_barrier((weights / denominator[..., None]).astype(jnp.bfloat16)).astype(jnp.float32)
        own_probs = lax.optimization_barrier((own_weights / denominator[..., None]).astype(jnp.bfloat16)).astype(jnp.float32)
        result = jnp.einsum('shk,khe->she', probs, cache_values) + jnp.einsum('sht,the->she', own_probs, own_values)
        return result.astype(jnp.bfloat16)
    attended = lax.map(slot_output, jnp.arange(slot_count, dtype=jnp.int32))
    return attended.reshape(slot_count, step_count, HEADS * HEAD)
```

```python
import functools
import math

import jax
import jax.numpy as jnp
from jax import lax
from jax.experimental import pallas as pl
from jax.experimental.pallas import tpu as pltpu
from jax.sharding import PartitionSpec as P

HEAD = 128
PAIR = 2
SLOTS = 4
NT = (((1,), (1,)), ((), ()))
VMEM_LIMIT = 48 * 1024 * 1024


def params():
    return pltpu.CompilerParams(vmem_limit_bytes=VMEM_LIMIT)


def split(values):
    high = values.astype(jnp.bfloat16)
    return high, (values - high.astype(jnp.float32)).astype(jnp.bfloat16)


def swap_gather(values, axis, size, index, perm):
    if size == 1:
        return values[None]
    other = lax.ppermute(values, axis, perm)
    first = index == 0
    return jnp.stack([jnp.where(first, values, other), jnp.where(first, other, values)])


def put_lanes(ref, rows, values):
    for tile in range(ref.shape[0]):
        part = values[:, tile * 128 : (tile + 1) * 128]
        if part.shape[1] < 128:
            fill = jnp.zeros((part.shape[0], 128 - part.shape[1]), part.dtype)
            part = jnp.concatenate([part, fill], axis=1)
        ref[tile, rows, :] = part


def take_lanes(ref, rows, width):
    tiles = [ref[tile, rows, :] for tile in range(ref.shape[0])]
    return jnp.concatenate(tiles, axis=1)[:, :width]


def absorb_kernel(heads, q_ref, weight_ref, gain_ref, out_ref, rows_ref):
    count = q_ref.shape[0]
    gain = gain_ref[...]
    for head in range(heads):
        lanes = pl.ds(head * HEAD, HEAD)
        mixed = lax.dot_general(
            q_ref[:, lanes], weight_ref[:, lanes], NT, preferred_element_type=jnp.float32
        )
        put_lanes(rows_ref, pl.ds(head, count, stride=heads), mixed * gain)
    out_ref[...] = take_lanes(rows_ref, slice(None), out_ref.shape[1]).astype(jnp.bfloat16)


def score_kernel(slots, per_slot, qk_ref, x_ref, slot_ref, out_ref):
    x = x_ref[...]
    tokens = x.shape[0]
    slot = jnp.broadcast_to(slot_ref[0], (per_slot, tokens))
    depth = SLOTS * per_slot

    def step(group, scores):
        start = pl.multiple_of(group * depth, depth)
        part = lax.dot_general(
            qk_ref[pl.ds(start, depth), :], x, NT, preferred_element_type=jnp.float32
        )
        for j in range(SLOTS):
            here = slot == group * SLOTS + j
            scores = jnp.where(here, part[j * per_slot : (j + 1) * per_slot], scores)
        return scores

    scores = lax.fori_loop(
        0, slots // SLOTS, step, jnp.zeros((per_slot, tokens), jnp.float32), unroll=True
    )
    values = x.astype(jnp.float32)
    high, low = split(values * values)
    ones = jnp.ones((8, x.shape[1]), jnp.bfloat16)
    total = lax.dot_general(ones, high, NT, preferred_element_type=jnp.float32)
    total = total + lax.dot_general(ones, low, NT, preferred_element_type=jnp.float32)
    total_high, total_low = split(total)
    row = lax.broadcasted_iota(jnp.int32, total.shape, 0)
    total = jnp.where(row == 0, total_high, jnp.where(row == 1, total_low, 0.0))
    out_ref[0] = jnp.concatenate([scores, total], axis=0).astype(jnp.bfloat16)


def value_kernel(
    slots, per_slot, heads, w_ref, x_ref, slot_ref, weight_ref, gain_ref, out_ref, d_ref,
    w_all, p_ref, mixed_ref,
):
    blocks, _, width = w_ref.shape
    for b in range(blocks):
        w_all[:, b * width : (b + 1) * width] = w_ref[b]
    tokens = blocks * width
    slot = slot_ref[...]
    one_hot = (
        lax.broadcasted_iota(jnp.int32, (slots, tokens), 0) == slot
    ).astype(jnp.float32).astype(jnp.bfloat16)
    weights = w_all[:per_slot, :]
    total = lax.dot_general(weights, one_hot, NT, preferred_element_type=jnp.float32)
    d_ref[...] = total
    inverse = jnp.where(total > 0.0, 1.0 / jnp.where(total > 0.0, total, 1.0), 0.0)
    high, low = split(inverse)
    scale = jnp.dot(high, one_hot, preferred_element_type=jnp.float32)
    scale = scale + jnp.dot(low, one_hot, preferred_element_type=jnp.float32)
    extra = w_all[per_slot:, :].astype(jnp.float32)
    factor = extra[0:1] + extra[1:2]
    p_ref[...] = (weights.astype(jnp.float32) * scale * factor).astype(jnp.bfloat16)
    depth = SLOTS * per_slot
    gain = gain_ref[...]
    x = x_ref[...]

    def step(group, carry):
        p = p_ref[...]
        zero = jnp.zeros_like(p)
        wide = jnp.broadcast_to(slot, p.shape)
        rows = [jnp.where(wide == group * SLOTS + j, p, zero) for j in range(SLOTS)]
        mixed = jnp.dot(
            jnp.concatenate(rows, axis=0), x, preferred_element_type=jnp.float32
        )
        put_lanes(mixed_ref, pl.ds(pl.multiple_of(group * depth, depth), depth), mixed * gain)
        return carry

    lax.fori_loop(0, slots // SLOTS, step, 0)
    count = out_ref.shape[0]
    for head in range(heads):
        rows = take_lanes(mixed_ref, pl.ds(head, count, stride=heads), x.shape[1])
        rows = rows.astype(jnp.bfloat16)
        lanes = pl.ds(head * HEAD, HEAD)
        out_ref[:, lanes] = jnp.dot(
            rows, weight_ref[:, lanes], preferred_element_type=jnp.float32
        ).astype(jnp.bfloat16)


def on_device(
    slab, token_request, request_slot, new_states, cache_gain, query_gain,
    key_weight, value_weight, query_weight,
):
    f32, bf16 = jnp.float32, jnp.bfloat16
    seq, tp = lax.axis_size("seq"), lax.axis_size("tp")
    k, c = lax.axis_index("seq"), lax.axis_index("tp")
    tokens, half = slab.shape
    model = half * tp
    own = tokens // tp
    feat = model // seq
    pair = PAIR if seq % PAIR == 0 else 1
    shards = seq // pair
    wide = feat * pair
    x, m = k % pair, k // pair
    groups = [[pair * i + p for i in range(shards)] for p in range(pair)]
    x_perm = [(i, i ^ 1) for i in range(seq)]
    tp_perm = [(0, 1), (1, 0)]
    local_width = key_weight.shape[1]
    heads_local = local_width // HEAD
    heads = heads_local * tp
    per, steps, _ = new_states.shape
    slots = request_slot.shape[0]
    own_rows = per * steps
    rows = slots * steps
    per_slot = steps * heads
    scale = 1.0 / math.sqrt(HEAD)

    def over_tp(values):
        if tp == 2:
            return swap_gather(values, "tp", tp, c, tp_perm)
        return lax.all_gather(values, "tp", axis=0, tiled=False)

    cut = slab.reshape(tp, own, half)
    if tp == 2:
        mine = lax.dynamic_index_in_dim(cut, c, 0, keepdims=False)
        other = lax.ppermute(
            lax.dynamic_index_in_dim(cut, 1 - c, 0, keepdims=False), "tp", tp_perm
        )
        whole = jnp.stack([jnp.where(c == 0, mine, other), jnp.where(c == 0, other, mine)])
    else:
        whole = lax.all_to_all(cut, "tp", 0, 0, tiled=True)
    message = whole.reshape(tp, own, shards // tp, wide).transpose(0, 2, 1, 3)
    slab_in = lax.all_to_all(
        message.reshape(shards, own, wide), "seq", 0, 0, tiled=True, axis_index_groups=groups
    )

    requests = lax.dynamic_index_in_dim(token_request.reshape(tp, own), c, 0, keepdims=False)
    match = requests[None, :] == jnp.arange(slots, dtype=jnp.int32)[:, None]
    target = jnp.sum(jnp.where(match, request_slot[:, None], 0), axis=0)
    states = over_tp(new_states.reshape(own_rows, half)).transpose(1, 0, 2).reshape(own_rows, model)
    squares = states.astype(f32)
    own_factor = lax.rsqrt(jnp.mean(squares * squares, axis=-1, keepdims=True) + 1e-06)
    slot_rows = -(-own // feat)
    carried = jnp.pad(target.astype(bf16), (0, slot_rows * feat - own)).reshape(slot_rows, feat)
    sent = jnp.concatenate(
        [
            states.reshape(own_rows, seq, feat).transpose(1, 0, 2),
            jnp.broadcast_to(carried[None], (seq, slot_rows, feat)),
        ],
        axis=1,
    )
    got = lax.all_to_all(sent, "seq", 0, 0, tiled=True)
    state_part = got[:, :own_rows].reshape(rows, feat)
    slots_in = got[:, own_rows:].reshape(shards, pair, slot_rows * feat)[:, :, :own]
    slots_in = lax.dynamic_index_in_dim(slots_in, x, 1, keepdims=False).astype(jnp.int32)

    query_part = lax.dynamic_slice(query_gain, (k * feat,), (feat,))
    gained = (state_part.astype(f32) * query_part[None]).astype(bf16)
    partial = jnp.dot(gained, query_weight, preferred_element_type=f32).astype(bf16)
    partial = lax.all_to_all(
        partial.reshape(seq, own_rows, local_width), "seq", 0, 0, tiled=True
    )
    query = (jnp.sum(partial.astype(f32), axis=0) * own_factor).astype(bf16)
    queries = lax.all_to_all(
        jnp.broadcast_to(query[None], (seq, own_rows, local_width)), "seq", 0, 0, tiled=True
    ).reshape(rows, local_width)
    queries = over_tp(queries).transpose(1, 0, 2).reshape(rows, heads * HEAD)

    def gather_rows(weight):
        block = swap_gather(weight, "seq", pair, x, x_perm).reshape(wide, local_width)
        return over_tp(block).transpose(1, 0, 2).reshape(wide, heads * HEAD)

    keys_full, values_full = gather_rows(key_weight), gather_rows(value_weight)
    gain = lax.dynamic_slice(cache_gain, (m * wide,), (wide,)).reshape(1, wide)
    absorbed = pl.pallas_call(
        functools.partial(absorb_kernel, heads),
        out_shape=jax.ShapeDtypeStruct((rows * heads, wide), bf16),
        scratch_shapes=[pltpu.VMEM((-(-wide // 128), rows * heads, 128), f32)],
        compiler_params=params(),
        name="absorb",
    )(queries, keys_full, gain)

    new_cols = rows // shards
    width = -(-(own + new_cols) // 128) * 128
    state_wide = swap_gather(state_part, "seq", pair, x, x_perm)
    state_wide = state_wide.transpose(1, 0, 2).reshape(shards, new_cols, wide)
    tokens_in = jnp.concatenate(
        [slab_in, jnp.pad(state_wide, ((0, 0), (0, width - own - new_cols), (0, 0)))], axis=1
    ).reshape(shards * width, wide)

    group = x * tp + c
    new_slot = jnp.arange(rows, dtype=jnp.int32) // steps
    new_slot = jnp.where(new_slot % (pair * tp) == group, new_slot, -1).reshape(shards, new_cols)
    slot_in = jnp.concatenate(
        [slots_in, new_slot, jnp.full((shards, width - own - new_cols), -1, jnp.int32)], axis=1
    )

    out_rows = per_slot + 8
    partial = pl.pallas_call(
        functools.partial(score_kernel, slots, per_slot),
        grid=(shards,),
        in_specs=[
            pl.BlockSpec((rows * heads, wide), lambda i: (0, 0)),
            pl.BlockSpec((width, wide), lambda i: (i, 0)),
            pl.BlockSpec((1, 1, width), lambda i: (i, 0, 0)),
        ],
        out_specs=pl.BlockSpec((1, out_rows, width), lambda i: (i, 0, 0)),
        out_shape=jax.ShapeDtypeStruct((shards, out_rows, width), bf16),
        compiler_params=params(),
        name="scores",
    )(absorbed, tokens_in, slot_in.reshape(shards, 1, width))
    partial = lax.all_to_all(partial, "seq", 0, 0, tiled=True, axis_index_groups=groups)
    summed = jnp.sum(partial.astype(f32), axis=0)
    mean = (summed[per_slot] + summed[per_slot + 1]) / model
    factor = lax.rsqrt(mean + 1e-06)[None]
    my_slot = lax.dynamic_index_in_dim(slot_in, m, 0, keepdims=True)
    column = jnp.arange(width, dtype=jnp.int32)[None]
    step_of = jnp.arange(per_slot, dtype=jnp.int32)[:, None] // heads
    seen = (my_slot >= 0) & ((column < own) | ((column - own) % steps <= step_of))
    weights = jnp.where(seen, jnp.exp(summed[:per_slot] * (factor * scale)), 0.0)
    high, low = split(factor)
    ready = jnp.concatenate(
        [weights.astype(bf16), high, low, jnp.zeros((6, width), bf16)], axis=0
    )
    weights_in = lax.all_to_all(
        jnp.broadcast_to(ready[None], (shards, out_rows, width)),
        "seq", 0, 0, tiled=True, axis_index_groups=groups,
    )

    attended, totals = pl.pallas_call(
        functools.partial(value_kernel, slots, per_slot, heads),
        out_shape=(
            jax.ShapeDtypeStruct((rows, heads * HEAD), bf16),
            jax.ShapeDtypeStruct((per_slot, slots), f32),
        ),
        scratch_shapes=[
            pltpu.VMEM((out_rows, shards * width), bf16),
            pltpu.VMEM((per_slot, shards * width), bf16),
            pltpu.VMEM((-(-wide // 128), rows * heads, 128), f32),
        ],
        compiler_params=params(),
        name="values",
    )(weights_in, tokens_in, slot_in.reshape(1, shards * width), values_full, gain)

    totals = totals.T.reshape(seq, per, steps, tp, heads_local).transpose(0, 3, 1, 2, 4)
    totals = totals.reshape(seq, tp, 1, own_rows * heads_local)
    totals = jnp.concatenate(split(totals), axis=2)
    parts = attended.reshape(seq, own_rows, tp, local_width).transpose(0, 2, 1, 3)
    spare = local_width - own_rows * heads_local
    sent = jnp.concatenate([parts, jnp.pad(totals, ((0, 0), (0, 0), (0, 0), (0, spare)))], axis=2)
    got = lax.all_to_all(
        sent.reshape(seq * tp, own_rows + 2, local_width), ("seq", "tp"), 0, 0, tiled=True
    ).reshape(shards, pair, tp, own_rows + 2, local_width).astype(f32)
    sums = jnp.sum(got[:, :, :, :own_rows], axis=0)
    share = got[0, :, :, own_rows, :] + got[0, :, :, own_rows + 1, :]
    share = share[..., : own_rows * heads_local].reshape(pair, tp, own_rows, heads_local)
    share = share / jnp.sum(share, axis=(0, 1), keepdims=True)
    sums = sums.reshape(pair, tp, own_rows, heads_local, HEAD) * share[..., None]
    return jnp.sum(sums, axis=(0, 1)).reshape(per, steps, local_width).astype(bf16)


def solution(mesh):
    placed = (
        P("seq", "tp"),
        P("seq", None),
        P(),
        P("seq", None, "tp"),
        P(),
        P(),
        P("seq", "tp"),
        P("seq", "tp"),
        P("seq", "tp"),
    )
    return jax.shard_map(
        on_device, mesh=mesh, in_specs=placed, out_specs=P("seq", None, "tp"), check_vma=False
    )
```

```python
import functools
import math

import jax
import jax.numpy as jnp
from jax import lax
from jax.experimental import pallas as pl
from jax.experimental.pallas import tpu as pltpu
from jax.sharding import PartitionSpec as P

HEAD = 128
PAIR = 2
SLOTS = 4
BLOCKS = 4
NT = (((1,), (1,)), ((), ()))
VMEM_LIMIT = 48 * 1024 * 1024


def params():
    return pltpu.CompilerParams(vmem_limit_bytes=VMEM_LIMIT)


def split(values):
    high = values.astype(jnp.bfloat16)
    return high, (values - high.astype(jnp.float32)).astype(jnp.bfloat16)


def halves(values):
    high = lax.reduce_precision(values, 8, 7)
    return high.astype(jnp.bfloat16), (values - high).astype(jnp.bfloat16)


def thirds(values):
    high = lax.reduce_precision(values, 8, 7)
    return high.astype(jnp.bfloat16), *halves(values - high)


def swap_gather(values, axis, size, index, perm):
    if size == 1:
        return values[None]
    other = lax.ppermute(values, axis, perm)
    first = index == 0
    return jnp.stack([jnp.where(first, values, other), jnp.where(first, other, values)])


def put_lanes(ref, rows, values):
    for tile in range(ref.shape[0]):
        part = values[:, tile * 128 : (tile + 1) * 128]
        if part.shape[1] < 128:
            fill = jnp.zeros((part.shape[0], 128 - part.shape[1]), part.dtype)
            part = jnp.concatenate([part, fill], axis=1)
        ref[tile, rows, :] = part


def take_lanes(ref, rows, width):
    tiles = [ref[tile, rows, :] for tile in range(ref.shape[0])]
    return jnp.concatenate(tiles, axis=1)[:, :width]


def absorb_kernel(count, *refs):
    queries, weights = refs[:count], refs[count : 2 * count]
    gain_ref, out_ref, rows_ref = refs[2 * count :]
    rows, per = queries[0].shape[0], queries[0].shape[1] // HEAD
    gain = gain_ref[...]
    for piece in range(count):
        for head in range(per):
            lanes = pl.ds(head * HEAD, HEAD)
            mixed = lax.dot_general(
                queries[piece][:, lanes], weights[piece][:, lanes], NT,
                preferred_element_type=jnp.float32,
            )
            place = pl.ds(piece * per + head, rows, stride=count * per)
            put_lanes(rows_ref, place, mixed * gain)
    out_ref[...] = take_lanes(rows_ref, slice(None), out_ref.shape[1]).astype(jnp.bfloat16)


def score_tile(slots, per_slot, qk_ref, x, slot):
    tokens = x.shape[0]
    slot = jnp.broadcast_to(slot, (per_slot, tokens))
    depth = SLOTS * per_slot
    scores = jnp.zeros((per_slot, tokens), jnp.float32)
    for group in range(slots // SLOTS):
        part = lax.dot_general(
            qk_ref[group * depth : (group + 1) * depth, :], x, NT,
            preferred_element_type=jnp.float32,
        )
        for j in range(SLOTS):
            here = slot == group * SLOTS + j
            scores = jnp.where(here, part[j * per_slot : (j + 1) * per_slot], scores)
    values = x.astype(jnp.float32)
    high, low = split(values * values)
    ones = jnp.ones((8, x.shape[1]), jnp.bfloat16)
    total = lax.dot_general(ones, high, NT, preferred_element_type=jnp.float32)
    total = total + lax.dot_general(ones, low, NT, preferred_element_type=jnp.float32)
    total_high, total_low = split(total)
    row = lax.broadcasted_iota(jnp.int32, total.shape, 0)
    total = jnp.where(
        row == 0, total_high.astype(jnp.float32), jnp.where(row == 1, total_low.astype(jnp.float32), 0.0)
    )
    return jnp.concatenate([scores, total], axis=0).astype(jnp.bfloat16)


def score_kernel(
    slots, per_slot, new_cols, qk_ref, slot_ref, new_slot_ref, slab_ref, new_ref, out_ref
):
    shards, own, wide = slab_ref.shape
    new = score_tile(slots, per_slot, qk_ref, new_ref[...], new_slot_ref[...])
    batch = BLOCKS if shards % BLOCKS == 0 else 1
    for first in range(0, shards, batch):
        x = slab_ref[first : first + batch].reshape(batch * own, wide)
        slot = slot_ref[:, first * own : (first + batch) * own]
        tile = score_tile(slots, per_slot, qk_ref, x, slot)
        for i in range(batch):
            out_ref[first + i, :, 0:own] = tile[:, i * own : (i + 1) * own]
    for place in range(shards):
        out_ref[place, :, own : own + new_cols] = new[:, place * new_cols : (place + 1) * new_cols]
        rest = out_ref.shape[2] - own - new_cols
        out_ref[place, :, own + new_cols :] = jnp.zeros((per_slot + 8, rest), jnp.bfloat16)


def value_kernel(
    slots, per_slot, new_cols, count, w_ref, slot_ref, gain_ref, slab_ref, new_ref, *refs
):
    weights_in, outs = refs[:count], refs[count : 2 * count]
    d_ref, x_ref, w_all, p_ref, mixed_ref = refs[2 * count :]
    shards, own, _ = slab_ref.shape
    tokens = w_all.shape[1]
    w_all[:, shards * own :] = jnp.zeros((per_slot + 8, tokens - shards * own), jnp.bfloat16)
    for b in range(shards):
        x_ref[b * own : (b + 1) * own, :] = slab_ref[b]
        w_all[:, b * own : (b + 1) * own] = w_ref[b, :, 0:own]
        start = shards * own + b * new_cols
        w_all[:, start : start + new_cols] = w_ref[b, :, own : own + new_cols]
    x_ref[shards * own :, :] = new_ref[...]
    slot = slot_ref[...]
    one_hot = (
        lax.broadcasted_iota(jnp.int32, (slots, tokens), 0) == slot
    ).astype(jnp.float32).astype(jnp.bfloat16)
    weights = w_all[:per_slot, :]
    total = lax.dot_general(weights, one_hot, NT, preferred_element_type=jnp.float32)
    by_slot = lax.dot_general(one_hot, weights, NT, preferred_element_type=jnp.float32)
    steps = d_ref.shape[0] // slots
    heads = per_slot // steps
    fill = jnp.zeros((slots, 128 - heads), jnp.float32)
    for step_id in range(steps):
        part = by_slot[:, step_id * heads : (step_id + 1) * heads]
        d_ref[pl.ds(step_id, slots, stride=steps), :] = jnp.concatenate([part, fill], axis=1)
    inverse = jnp.where(total > 0.0, 1.0 / jnp.where(total > 0.0, total, 1.0), 0.0)
    high, low = split(inverse)
    scale = jnp.dot(high, one_hot, preferred_element_type=jnp.float32)
    scale = scale + jnp.dot(low, one_hot, preferred_element_type=jnp.float32)
    extra = w_all[per_slot:, :].astype(jnp.float32)
    factor = extra[0:1] + extra[1:2]
    p_ref[...] = weights.astype(jnp.float32) * scale * factor
    depth = SLOTS * per_slot
    gain = gain_ref[...]

    def step(group, carry):
        p = p_ref[...]
        wide = jnp.broadcast_to(slot, p.shape)
        rows = [jnp.where(wide == group * SLOTS + j, p, 0.0) for j in range(SLOTS)]
        mixed = jnp.dot(
            jnp.concatenate(rows, axis=0).astype(jnp.bfloat16), x_ref[...],
            preferred_element_type=jnp.float32,
        )
        put_lanes(mixed_ref, pl.ds(pl.multiple_of(group * depth, depth), depth), mixed * gain)
        return carry

    lax.fori_loop(0, slots // SLOTS, step, 0, unroll=2)
    rows, per = outs[0].shape[0], outs[0].shape[1] // HEAD
    for piece in range(count):
        for head in range(per):
            place = pl.ds(piece * per + head, rows, stride=count * per)
            mixed = take_lanes(mixed_ref, place, x_ref.shape[1]).astype(jnp.bfloat16)
            lanes = pl.ds(head * HEAD, HEAD)
            outs[piece][:, lanes] = jnp.dot(
                mixed, weights_in[piece][:, lanes], preferred_element_type=jnp.float32
            ).astype(jnp.bfloat16)


def join_kernel(own_rows, part_ref, theirs_ref, d_ref, theirs_d_ref, out_ref):
    rows, width = part_ref.shape
    heads = width // HEAD
    mine, theirs = d_ref[:, :heads], theirs_d_ref[:, heads : 2 * heads]
    joined = mine + theirs
    inverse = jnp.where(joined > 0.0, 1.0 / jnp.where(joined > 0.0, joined, 1.0), 0.0)
    mine, theirs = mine * inverse, theirs * inverse
    joined = jnp.concatenate([joined, jnp.zeros((rows, 128 - heads), jnp.float32)], axis=1)
    high, low = split(joined)
    high, low = high.astype(jnp.float32), low.astype(jnp.float32)
    for head in range(heads):
        lanes = pl.ds(head * HEAD, HEAD)
        value = part_ref[:, lanes].astype(jnp.float32) * mine[:, head : head + 1]
        value = value + theirs_ref[:, lanes].astype(jnp.float32) * theirs[:, head : head + 1]
        for i in range(rows // own_rows):
            if head < own_rows:
                row = slice(i * own_rows + head, i * own_rows + head + 1)
                extra = [high[row], low[row]]
            else:
                extra = [jnp.zeros((2, HEAD), jnp.float32)]
            block = jnp.concatenate([value[i * own_rows : (i + 1) * own_rows]] + extra, axis=0)
            out_ref[i, :, lanes] = block.astype(jnp.bfloat16)


def on_device(
    slab, token_request, request_slot, new_states, cache_gain, query_gain,
    key_weight, value_weight, query_weight,
):
    f32, bf16 = jnp.float32, jnp.bfloat16
    seq, tp = lax.axis_size("seq"), lax.axis_size("tp")
    k, c = lax.axis_index("seq"), lax.axis_index("tp")
    tokens, half = slab.shape
    model = half * tp
    own = tokens // tp
    feat = model // seq
    pair = PAIR if seq % PAIR == 0 else 1
    shards = seq // pair
    wide = feat * pair
    x, m = k % pair, k // pair
    groups = [[pair * i + p for i in range(shards)] for p in range(pair)]
    x_perm = [(i, i ^ 1) for i in range(seq)]
    tp_perm = [(0, 1), (1, 0)]
    local_width = key_weight.shape[1]
    heads_local = local_width // HEAD
    heads = heads_local * tp
    per, steps, _ = new_states.shape
    slots = request_slot.shape[0]
    own_rows = per * steps
    rows = slots * steps
    per_slot = steps * heads
    scale = 1.0 / math.sqrt(HEAD)

    def over_tp(values):
        if tp == 2:
            return [values, lax.ppermute(values, "tp", tp_perm)]
        everyone = lax.all_gather(values, "tp", axis=0, tiled=False)
        return [everyone[i] for i in range(tp)]

    cut = slab.reshape(tp, own, half)
    if tp == 2:
        mine = lax.dynamic_index_in_dim(cut, c, 0, keepdims=False)
        other = lax.ppermute(
            lax.dynamic_index_in_dim(cut, 1 - c, 0, keepdims=False), "tp", tp_perm
        )
        whole = jnp.stack([jnp.where(c == 0, mine, other), jnp.where(c == 0, other, mine)])
    else:
        whole = lax.all_to_all(cut, "tp", 0, 0, tiled=True)
    message = whole.reshape(tp, own, shards // tp, wide).transpose(0, 2, 1, 3)
    message = message.reshape(shards, own, wide)

    requests = lax.dynamic_index_in_dim(token_request.reshape(tp, own), c, 0, keepdims=False)
    match = requests[None, :] == jnp.arange(slots, dtype=jnp.int32)[:, None]
    target = jnp.sum(jnp.where(match, request_slot[:, None], 0), axis=0)
    states = over_tp(new_states.reshape(own_rows, half))
    if tp == 2:
        states = [jnp.where(c == 0, states[i], states[1 - i]) for i in range(2)]
    states = jnp.concatenate(states, axis=1)
    squares = states.astype(f32)
    own_factor = lax.rsqrt(jnp.mean(squares * squares, axis=-1, keepdims=True) + 1e-06)
    carried = jnp.concatenate([target.astype(bf16), *thirds(own_factor[:, 0])])
    carried_rows = -(-carried.shape[0] // feat)
    carried = jnp.pad(carried, (0, carried_rows * feat - carried.shape[0]))
    carried = jnp.broadcast_to(carried.reshape(1, carried_rows, feat), (seq, carried_rows, feat))
    sent = jnp.concatenate(
        [states.reshape(own_rows, seq, feat).transpose(1, 0, 2), carried], axis=1
    )
    got = lax.all_to_all(sent, "seq", 0, 0, tiled=True)
    state_part = got[:, :own_rows].reshape(rows, feat)
    carried = got[:, own_rows:].reshape(seq, carried_rows * feat)
    slots_in = carried[:, :own].reshape(shards, pair, own)
    slots_in = lax.dynamic_index_in_dim(slots_in, x, 1, keepdims=False).astype(jnp.int32)
    row_factor = carried[:, own : own + 3 * own_rows].astype(f32).reshape(seq, 3, own_rows)
    row_factor = (row_factor[:, 0] + row_factor[:, 1] + row_factor[:, 2]).reshape(rows, 1)

    exchange = functools.partial(
        lax.all_to_all, axis_name="seq", split_axis=0, concat_axis=0, tiled=True,
        axis_index_groups=groups,
    )
    gain_part = lax.dynamic_slice(query_gain, (k * feat,), (feat,))
    query_part = (state_part.astype(f32) * row_factor * gain_part).astype(bf16)
    partial = jnp.dot(query_part, query_weight, preferred_element_type=f32)
    partial = partial.reshape(seq, own_rows, local_width)
    partial = partial.astype(bf16)
    partial = lax.all_to_all(partial, "seq", 0, 0, tiled=True)
    query = jnp.sum(partial.astype(f32), axis=0).astype(bf16)
    queries = lax.all_to_all(
        jnp.broadcast_to(query[None], (seq, own_rows, local_width)), "seq", 0, 0, tiled=True
    ).reshape(rows, local_width)
    state_wide = swap_gather(state_part, "seq", pair, x, x_perm)
    queries, state_wide, message, key_weight, value_weight = lax.optimization_barrier(
        (queries, state_wide, message, key_weight, value_weight)
    )
    slab_in = exchange(message)
    queries = over_tp(queries)

    def join_pair(first, second):
        if pair == 1:
            return first
        low = x == 0
        return jnp.concatenate(
            [jnp.where(low, first, second), jnp.where(low, second, first)], axis=0
        )

    def from_pair(values):
        return values if pair == 1 else lax.ppermute(values, "seq", x_perm)

    keys_full = over_tp(join_pair(key_weight, from_pair(key_weight)))
    value_other = from_pair(value_weight)
    gain = lax.dynamic_slice(cache_gain, (m * wide,), (wide,)).reshape(1, wide)
    absorbed = pl.pallas_call(
        functools.partial(absorb_kernel, tp),
        out_shape=jax.ShapeDtypeStruct((rows * heads, wide), bf16),
        scratch_shapes=[pltpu.VMEM((-(-wide // 128), rows * heads, 128), f32)],
        compiler_params=params(),
        name="absorb",
    )(*queries, *keys_full, gain)

    new_cols = rows // shards
    width = -(-(own + new_cols) // 128) * 128
    new_width = -(-rows // 128) * 128
    state_wide = state_wide.transpose(1, 0, 2).reshape(rows, wide)
    state_wide = jnp.pad(state_wide, ((0, new_width - rows), (0, 0)))
    group = x * tp + c
    new_slot = jnp.arange(rows, dtype=jnp.int32) // steps
    new_slot = jnp.where(new_slot % (pair * tp) == group, new_slot, -1)
    slot_row = slots_in.reshape(1, shards * own)
    new_row = jnp.pad(new_slot, (0, new_width - rows), constant_values=-1)[None]
    out_rows = per_slot + 8
    partial = pl.pallas_call(
        functools.partial(score_kernel, slots, per_slot, new_cols),
        out_shape=jax.ShapeDtypeStruct((shards, out_rows, width), bf16),
        compiler_params=params(),
        name="scores",
    )(absorbed, slot_row, new_row, slab_in, state_wide)
    partial, value_other = lax.optimization_barrier((partial, value_other))
    partial = lax.all_to_all(partial, "seq", 0, 0, tiled=True, axis_index_groups=groups)
    values_full = over_tp(join_pair(value_weight, value_other))
    summed = jnp.sum(partial.astype(f32), axis=0)
    mean = (summed[per_slot] + summed[per_slot + 1]) / model
    factor = lax.rsqrt(mean + 1e-06)[None]
    my_new = lax.dynamic_slice(new_slot, (m * new_cols,), (new_cols,))
    spare = jnp.full((width - own - new_cols,), -1, jnp.int32)
    my_slot = jnp.concatenate([target, my_new, spare])[None]
    column = jnp.arange(width, dtype=jnp.int32)[None]
    step_of = jnp.arange(per_slot, dtype=jnp.int32)[:, None] // heads
    seen = (my_slot >= 0) & ((column < own) | ((column - own) % steps <= step_of))
    weights = jnp.where(seen, jnp.exp(summed[:per_slot] * (factor * scale)), 0.0)
    high, low = halves(factor)
    ready = jnp.concatenate(
        [weights.astype(bf16), high, low, jnp.zeros((6, width), bf16)], axis=0
    )
    weights_in = lax.all_to_all(
        jnp.broadcast_to(ready[None], (shards, out_rows, width)),
        "seq", 0, 0, tiled=True, axis_index_groups=groups,
    )

    tokens_all = shards * own + new_width
    *attended, totals = pl.pallas_call(
        functools.partial(value_kernel, slots, per_slot, new_cols, tp),
        out_shape=tuple(
            jax.ShapeDtypeStruct((rows, local_width), bf16) for _ in range(tp)
        ) + (jax.ShapeDtypeStruct((rows, 128), f32),),
        scratch_shapes=[
            pltpu.VMEM((tokens_all, wide), bf16),
            pltpu.VMEM((out_rows, tokens_all), bf16),
            pltpu.VMEM((per_slot, tokens_all), f32),
            pltpu.VMEM((-(-wide // 128), rows * heads, 128), f32),
        ],
        compiler_params=params(),
        name="values",
    )(
        weights_in, jnp.concatenate([slot_row, new_row], axis=1), gain, slab_in, state_wide,
        *values_full,
    )

    if tp == 2 and own_rows <= heads_local:
        sent = pl.pallas_call(
            functools.partial(join_kernel, own_rows),
            out_shape=jax.ShapeDtypeStruct((seq, own_rows + 2, local_width), bf16),
            compiler_params=params(),
            name="join",
        )(
            attended[0], lax.ppermute(attended[1], "tp", tp_perm),
            totals, lax.ppermute(totals, "tp", tp_perm),
        )
        axes, groups_in, stride = "seq", pair, HEAD
    else:
        parts = jnp.stack([part.reshape(seq, own_rows, local_width) for part in attended], axis=1)
        totals = totals[:, :heads].reshape(seq, own_rows, tp, heads_local).transpose(0, 2, 1, 3)
        totals = jnp.stack(halves(totals), axis=2).reshape(seq, tp, 2, own_rows * heads_local)
        spare = local_width - own_rows * heads_local
        totals = jnp.pad(totals, ((0, 0), (0, 0), (0, 0), (0, spare)))
        sent = jnp.concatenate([parts, totals], axis=2)
        sent = sent.reshape(seq * tp, own_rows + 2, local_width)
        axes, groups_in, stride = ("seq", "tp"), pair * tp, heads_local
    got = lax.all_to_all(sent, axes, 0, 0, tiled=True)
    got = got.reshape(shards, groups_in, own_rows + 2, local_width).astype(f32)
    sums = jnp.sum(got[:, :, :own_rows], axis=0)
    share = got[0, :, own_rows, :] + got[0, :, own_rows + 1, :]
    share = share[:, : own_rows * stride].reshape(groups_in, own_rows, stride)[..., :heads_local]
    share = share / jnp.sum(share, axis=0, keepdims=True)
    sums = sums.reshape(groups_in, own_rows, heads_local, HEAD) * share[..., None]
    return jnp.sum(sums, axis=0).reshape(per, steps, local_width).astype(bf16)


def solution(mesh):
    placed = (
        P("seq", "tp"),
        P("seq", None),
        P(),
        P("seq", None, "tp"),
        P(),
        P(),
        P("seq", "tp"),
        P("seq", "tp"),
        P("seq", "tp"),
    )
    return jax.shard_map(
        on_device, mesh=mesh, in_specs=placed, out_specs=P("seq", None, "tp"), check_vma=False
    )
```

```python
import functools
import math

import jax
import jax.numpy as jnp
from jax import lax
from jax.experimental import pallas as pl
from jax.experimental.pallas import tpu as pltpu
from jax.sharding import PartitionSpec as P

HEAD = 128
PAIR = 2
SLOTS = 4
BLOCKS = 4
NT = (((1,), (1,)), ((), ()))
VMEM_LIMIT = 26 * 1024 * 1024


def params():
    return pltpu.CompilerParams(vmem_limit_bytes=VMEM_LIMIT)


def split(values):
    high = values.astype(jnp.bfloat16)
    return high, (values - high.astype(jnp.float32)).astype(jnp.bfloat16)


def halves(values):
    high = lax.reduce_precision(values, 8, 7)
    return high.astype(jnp.bfloat16), (values - high).astype(jnp.bfloat16)


def thirds(values):
    high = lax.reduce_precision(values, 8, 7)
    return high.astype(jnp.bfloat16), *halves(values - high)


def swap_gather(values, axis, size, index, perm):
    if size == 1:
        return values[None]
    other = lax.ppermute(values, axis, perm)
    first = index == 0
    return jnp.stack([jnp.where(first, values, other), jnp.where(first, other, values)])


def put_lanes(ref, rows, values):
    for tile in range(ref.shape[0]):
        part = values[:, tile * 128 : (tile + 1) * 128]
        if part.shape[1] < 128:
            fill = jnp.zeros((part.shape[0], 128 - part.shape[1]), part.dtype)
            part = jnp.concatenate([part, fill], axis=1)
        ref[tile, rows, :] = part


def take_lanes(ref, rows, width):
    tiles = [ref[tile, rows, :] for tile in range(ref.shape[0])]
    return jnp.concatenate(tiles, axis=1)[:, :width]


def absorb_kernel(count, *refs):
    queries, weights = refs[:count], refs[count : 2 * count]
    gain_ref, out_ref, rows_ref = refs[2 * count :]
    rows, per = queries[0].shape[0], queries[0].shape[1] // HEAD
    gain = gain_ref[...]
    for piece in range(count):
        for head in range(per):
            lanes = pl.ds(head * HEAD, HEAD)
            mixed = lax.dot_general(
                queries[piece][:, lanes], weights[piece][:, lanes], NT,
                preferred_element_type=jnp.float32,
            )
            place = pl.ds(piece * per + head, rows, stride=count * per)
            put_lanes(rows_ref, place, mixed * gain)
    out_ref[...] = take_lanes(rows_ref, slice(None), out_ref.shape[1]).astype(jnp.bfloat16)


def score_tile(slots, per_slot, qk_ref, x, slot):
    tokens = x.shape[0]
    slot = jnp.broadcast_to(slot, (per_slot, tokens))
    depth = SLOTS * per_slot
    scores = jnp.zeros((per_slot, tokens), jnp.float32)
    for group in range(slots // SLOTS):
        part = lax.dot_general(
            qk_ref[group * depth : (group + 1) * depth, :], x, NT,
            preferred_element_type=jnp.float32,
        )
        for j in range(SLOTS):
            here = slot == group * SLOTS + j
            scores = jnp.where(here, part[j * per_slot : (j + 1) * per_slot], scores)
    values = x.astype(jnp.float32)
    high, low = split(values * values)
    ones = jnp.ones((8, x.shape[1]), jnp.bfloat16)
    total = lax.dot_general(ones, high, NT, preferred_element_type=jnp.float32)
    total = total + lax.dot_general(ones, low, NT, preferred_element_type=jnp.float32)
    total_high, total_low = split(total)
    row = lax.broadcasted_iota(jnp.int32, total.shape, 0)
    total = jnp.where(
        row == 0, total_high.astype(jnp.float32), jnp.where(row == 1, total_low.astype(jnp.float32), 0.0)
    )
    return jnp.concatenate([scores, total], axis=0).astype(jnp.bfloat16)


def score_kernel(
    slots, per_slot, new_cols, qk_ref, slot_ref, new_slot_ref, slab_ref, new_ref, out_ref
):
    shards, own, wide = slab_ref.shape
    new = score_tile(slots, per_slot, qk_ref, new_ref[...], new_slot_ref[...])
    batch = BLOCKS if shards % BLOCKS == 0 else 1
    for first in range(0, shards, batch):
        x = slab_ref[first : first + batch].reshape(batch * own, wide)
        slot = slot_ref[:, first * own : (first + batch) * own]
        tile = score_tile(slots, per_slot, qk_ref, x, slot)
        for i in range(batch):
            out_ref[first + i, :, 0:own] = tile[:, i * own : (i + 1) * own]
    for place in range(shards):
        out_ref[place, :, own : own + new_cols] = new[:, place * new_cols : (place + 1) * new_cols]
        rest = out_ref.shape[2] - own - new_cols
        out_ref[place, :, own + new_cols :] = jnp.zeros((per_slot + 8, rest), jnp.bfloat16)


def value_kernel(
    slots, per_slot, new_cols, count, w_ref, slot_ref, gain_ref, slab_ref, new_ref, *refs
):
    weights_in, outs = refs[:count], refs[count : 2 * count]
    d_ref, x_ref, w_all, p_ref, mixed_ref = refs[2 * count :]
    shards, own, _ = slab_ref.shape
    tokens = w_all.shape[1]
    w_all[:, shards * own :] = jnp.zeros((per_slot + 8, tokens - shards * own), jnp.bfloat16)
    for b in range(shards):
        x_ref[b * own : (b + 1) * own, :] = slab_ref[b]
        w_all[:, b * own : (b + 1) * own] = w_ref[b, :, 0:own]
        start = shards * own + b * new_cols
        w_all[:, start : start + new_cols] = w_ref[b, :, own : own + new_cols]
    x_ref[shards * own :, :] = new_ref[...]
    slot = slot_ref[...]
    one_hot = (
        lax.broadcasted_iota(jnp.int32, (slots, tokens), 0) == slot
    ).astype(jnp.float32).astype(jnp.bfloat16)
    weights = w_all[:per_slot, :]
    total = lax.dot_general(weights, one_hot, NT, preferred_element_type=jnp.float32)
    by_slot = lax.dot_general(one_hot, weights, NT, preferred_element_type=jnp.float32)
    steps = d_ref.shape[0] // slots
    heads = per_slot // steps
    fill = jnp.zeros((slots, 128 - heads), jnp.float32)
    for step_id in range(steps):
        part = by_slot[:, step_id * heads : (step_id + 1) * heads]
        d_ref[pl.ds(step_id, slots, stride=steps), :] = jnp.concatenate([part, fill], axis=1)
    inverse = jnp.where(total > 0.0, 1.0 / jnp.where(total > 0.0, total, 1.0), 0.0)
    high, low = split(inverse)
    scale = jnp.dot(high, one_hot, preferred_element_type=jnp.float32)
    scale = scale + jnp.dot(low, one_hot, preferred_element_type=jnp.float32)
    extra = w_all[per_slot:, :].astype(jnp.float32)
    factor = extra[0:1] + extra[1:2]
    p_ref[...] = weights.astype(jnp.float32) * scale * factor
    depth = SLOTS * per_slot
    gain = gain_ref[...]

    def step(group, carry):
        p = p_ref[...]
        wide = jnp.broadcast_to(slot, p.shape)
        rows = [jnp.where(wide == group * SLOTS + j, p, 0.0) for j in range(SLOTS)]
        mixed = jnp.dot(
            jnp.concatenate(rows, axis=0).astype(jnp.bfloat16), x_ref[...],
            preferred_element_type=jnp.float32,
        )
        put_lanes(mixed_ref, pl.ds(pl.multiple_of(group * depth, depth), depth), mixed * gain)
        return carry

    lax.fori_loop(0, slots // SLOTS, step, 0, unroll=8)
    rows, per = outs[0].shape[0], outs[0].shape[1] // HEAD
    for piece in range(count):
        for head in range(per):
            place = pl.ds(piece * per + head, rows, stride=count * per)
            mixed = take_lanes(mixed_ref, place, x_ref.shape[1]).astype(jnp.bfloat16)
            lanes = pl.ds(head * HEAD, HEAD)
            outs[piece][:, lanes] = jnp.dot(
                mixed, weights_in[piece][:, lanes], preferred_element_type=jnp.float32
            ).astype(jnp.bfloat16)


def join_kernel(own_rows, part_ref, theirs_ref, d_ref, theirs_d_ref, out_ref):
    rows, width = part_ref.shape
    heads = width // HEAD
    mine, theirs = d_ref[:, :heads], theirs_d_ref[:, heads : 2 * heads]
    joined = mine + theirs
    inverse = jnp.where(joined > 0.0, 1.0 / jnp.where(joined > 0.0, joined, 1.0), 0.0)
    mine, theirs = mine * inverse, theirs * inverse
    joined = jnp.concatenate([joined, jnp.zeros((rows, 128 - heads), jnp.float32)], axis=1)
    high, low = split(joined)
    high, low = high.astype(jnp.float32), low.astype(jnp.float32)
    for head in range(heads):
        lanes = pl.ds(head * HEAD, HEAD)
        value = part_ref[:, lanes].astype(jnp.float32) * mine[:, head : head + 1]
        value = value + theirs_ref[:, lanes].astype(jnp.float32) * theirs[:, head : head + 1]
        for i in range(rows // own_rows):
            if head < own_rows:
                row = slice(i * own_rows + head, i * own_rows + head + 1)
                extra = [high[row], low[row]]
            else:
                extra = [jnp.zeros((2, HEAD), jnp.float32)]
            block = jnp.concatenate([value[i * own_rows : (i + 1) * own_rows]] + extra, axis=0)
            out_ref[i, :, lanes] = block.astype(jnp.bfloat16)


def on_device(
    slab, token_request, request_slot, new_states, cache_gain, query_gain,
    key_weight, value_weight, query_weight,
):
    f32, bf16 = jnp.float32, jnp.bfloat16
    seq, tp = lax.axis_size("seq"), lax.axis_size("tp")
    k, c = lax.axis_index("seq"), lax.axis_index("tp")
    tokens, half = slab.shape
    model = half * tp
    own = tokens // tp
    feat = model // seq
    pair = PAIR if seq % PAIR == 0 else 1
    shards = seq // pair
    wide = feat * pair
    x, m = k % pair, k // pair
    groups = [[pair * i + p for i in range(shards)] for p in range(pair)]
    x_perm = [(i, i ^ 1) for i in range(seq)]
    tp_perm = [(0, 1), (1, 0)]
    local_width = key_weight.shape[1]
    heads_local = local_width // HEAD
    heads = heads_local * tp
    per, steps, _ = new_states.shape
    slots = request_slot.shape[0]
    own_rows = per * steps
    rows = slots * steps
    per_slot = steps * heads
    scale = 1.0 / math.sqrt(HEAD)

    def over_tp(values):
        if tp == 2:
            return [values, lax.ppermute(values, "tp", tp_perm)]
        everyone = lax.all_gather(values, "tp", axis=0, tiled=False)
        return [everyone[i] for i in range(tp)]

    cut = slab.reshape(tp, own, half)
    if tp == 2:
        mine = lax.dynamic_index_in_dim(cut, c, 0, keepdims=False)
        other = lax.ppermute(
            lax.dynamic_index_in_dim(cut, 1 - c, 0, keepdims=False), "tp", tp_perm
        )
        whole = jnp.stack([jnp.where(c == 0, mine, other), jnp.where(c == 0, other, mine)])
    else:
        whole = lax.all_to_all(cut, "tp", 0, 0, tiled=True)
    message = whole.reshape(tp, own, shards // tp, wide).transpose(0, 2, 1, 3)
    message = message.reshape(shards, own, wide)

    requests = lax.dynamic_index_in_dim(token_request.reshape(tp, own), c, 0, keepdims=False)
    match = requests[None, :] == jnp.arange(slots, dtype=jnp.int32)[:, None]
    target = jnp.sum(jnp.where(match, request_slot[:, None], 0), axis=0)
    states = over_tp(new_states.reshape(own_rows, half))
    if tp == 2:
        states = [jnp.where(c == 0, states[i], states[1 - i]) for i in range(2)]
    states = jnp.concatenate(states, axis=1)
    squares = states.astype(f32)
    own_factor = lax.rsqrt(jnp.mean(squares * squares, axis=-1, keepdims=True) + 1e-06)
    carried = jnp.concatenate([target.astype(bf16), *thirds(own_factor[:, 0])])
    carried_rows = -(-carried.shape[0] // feat)
    carried = jnp.pad(carried, (0, carried_rows * feat - carried.shape[0]))
    carried = jnp.broadcast_to(carried.reshape(1, carried_rows, feat), (seq, carried_rows, feat))
    sent = jnp.concatenate(
        [states.reshape(own_rows, seq, feat).transpose(1, 0, 2), carried], axis=1
    )
    got = lax.all_to_all(sent, "seq", 0, 0, tiled=True)
    state_part = got[:, :own_rows].reshape(rows, feat)
    carried = got[:, own_rows:].reshape(seq, carried_rows * feat)
    slots_in = carried[:, :own].reshape(shards, pair, own)
    slots_in = lax.dynamic_index_in_dim(slots_in, x, 1, keepdims=False).astype(jnp.int32)
    row_factor = carried[:, own : own + 3 * own_rows].astype(f32).reshape(seq, 3, own_rows)
    row_factor = (row_factor[:, 0] + row_factor[:, 1] + row_factor[:, 2]).reshape(rows, 1)

    exchange = functools.partial(
        lax.all_to_all, axis_name="seq", split_axis=0, concat_axis=0, tiled=True,
        axis_index_groups=groups,
    )
    gain_part = lax.dynamic_slice(query_gain, (k * feat,), (feat,))
    query_part = (state_part.astype(f32) * row_factor * gain_part).astype(bf16)
    partial = jnp.dot(query_part, query_weight, preferred_element_type=f32)
    partial = partial.reshape(seq, own_rows, local_width)
    partial = partial.astype(bf16)
    partial = lax.all_to_all(partial, "seq", 0, 0, tiled=True)
    query = jnp.sum(partial.astype(f32), axis=0).astype(bf16)
    queries = exchange(jnp.broadcast_to(query[None], (shards, own_rows, local_width)))
    state_wide = swap_gather(state_part, "seq", pair, x, x_perm)
    queries, state_wide, message, key_weight, value_weight = lax.optimization_barrier(
        (queries, state_wide, message, key_weight, value_weight)
    )
    slab_in = exchange(message)
    queries = swap_gather(queries, "seq", pair, x, x_perm)
    queries = queries.transpose(1, 0, 2, 3).reshape(rows, local_width)
    queries = over_tp(queries)

    def join_pair(first, second):
        if pair == 1:
            return first
        low = x == 0
        return jnp.concatenate(
            [jnp.where(low, first, second), jnp.where(low, second, first)], axis=0
        )

    def from_pair(values):
        return values if pair == 1 else lax.ppermute(values, "seq", x_perm)

    keys_full = over_tp(join_pair(key_weight, from_pair(key_weight)))
    value_other = from_pair(value_weight)
    gain = lax.dynamic_slice(cache_gain, (m * wide,), (wide,)).reshape(1, wide)
    absorbed = pl.pallas_call(
        functools.partial(absorb_kernel, tp),
        out_shape=jax.ShapeDtypeStruct((rows * heads, wide), bf16),
        scratch_shapes=[pltpu.VMEM((-(-wide // 128), rows * heads, 128), f32)],
        compiler_params=params(),
        cost_estimate=pl.CostEstimate(
            flops=2 * rows * heads * HEAD * wide,
            bytes_accessed=2 * (wide + rows) * heads * HEAD,
            transcendentals=0,
        ),
        name="absorb",
    )(*queries, *keys_full, gain)

    new_cols = rows // shards
    width = -(-(own + new_cols) // 128) * 128
    new_width = -(-rows // 128) * 128
    state_wide = state_wide.transpose(1, 0, 2).reshape(rows, wide)
    state_wide = jnp.pad(state_wide, ((0, new_width - rows), (0, 0)))
    group = x * tp + c
    new_slot = jnp.arange(rows, dtype=jnp.int32) // steps
    new_slot = jnp.where(new_slot % (pair * tp) == group, new_slot, -1)
    slot_row = slots_in.reshape(1, shards * own)
    new_row = jnp.pad(new_slot, (0, new_width - rows), constant_values=-1)[None]
    out_rows = per_slot + 8
    partial = pl.pallas_call(
        functools.partial(score_kernel, slots, per_slot, new_cols),
        out_shape=jax.ShapeDtypeStruct((shards, out_rows, width), bf16),
        compiler_params=params(),
        name="scores",
    )(absorbed, slot_row, new_row, slab_in, state_wide)
    partial, value_other = lax.optimization_barrier((partial, value_other))
    partial = lax.all_to_all(partial, "seq", 0, 0, tiled=True, axis_index_groups=groups)
    values_full = over_tp(join_pair(value_weight, value_other))
    summed = jnp.sum(partial.astype(f32), axis=0)
    mean = (summed[per_slot] + summed[per_slot + 1]) / model
    factor = lax.rsqrt(mean + 1e-06)[None]
    my_new = lax.dynamic_slice(new_slot, (m * new_cols,), (new_cols,))
    spare = jnp.full((width - own - new_cols,), -1, jnp.int32)
    my_slot = jnp.concatenate([target, my_new, spare])[None]
    column = jnp.arange(width, dtype=jnp.int32)[None]
    step_of = jnp.arange(per_slot, dtype=jnp.int32)[:, None] // heads
    seen = (my_slot >= 0) & ((column < own) | ((column - own) % steps <= step_of))
    weights = jnp.where(seen, jnp.exp(summed[:per_slot] * (factor * scale)), 0.0)
    high, low = halves(factor)
    ready = jnp.concatenate(
        [weights.astype(bf16), high, low, jnp.zeros((6, width), bf16)], axis=0
    )
    weights_in = lax.all_to_all(
        jnp.broadcast_to(ready[None], (shards, out_rows, width)),
        "seq", 0, 0, tiled=True, axis_index_groups=groups,
    )

    tokens_all = shards * own + new_width
    *attended, totals = pl.pallas_call(
        functools.partial(value_kernel, slots, per_slot, new_cols, tp),
        out_shape=tuple(
            jax.ShapeDtypeStruct((rows, local_width), bf16) for _ in range(tp)
        ) + (jax.ShapeDtypeStruct((rows, 128), f32),),
        scratch_shapes=[
            pltpu.VMEM((tokens_all, wide), bf16),
            pltpu.VMEM((out_rows, tokens_all), bf16),
            pltpu.VMEM((per_slot, tokens_all), f32),
            pltpu.VMEM((-(-wide // 128), rows * heads, 128), f32),
        ],
        compiler_params=params(),
        name="values",
    )(
        weights_in, jnp.concatenate([slot_row, new_row], axis=1), gain, slab_in, state_wide,
        *values_full,
    )

    if tp == 2 and own_rows <= heads_local:
        sent = pl.pallas_call(
            functools.partial(join_kernel, own_rows),
            out_shape=jax.ShapeDtypeStruct((seq, own_rows + 2, local_width), bf16),
            compiler_params=params(),
            name="join",
        )(
            attended[0], lax.ppermute(attended[1], "tp", tp_perm),
            totals, lax.ppermute(totals, "tp", tp_perm),
        )
        axes, groups_in, stride = "seq", pair, HEAD
    else:
        parts = jnp.stack([part.reshape(seq, own_rows, local_width) for part in attended], axis=1)
        totals = totals[:, :heads].reshape(seq, own_rows, tp, heads_local).transpose(0, 2, 1, 3)
        totals = jnp.stack(halves(totals), axis=2).reshape(seq, tp, 2, own_rows * heads_local)
        spare = local_width - own_rows * heads_local
        totals = jnp.pad(totals, ((0, 0), (0, 0), (0, 0), (0, spare)))
        sent = jnp.concatenate([parts, totals], axis=2)
        sent = sent.reshape(seq * tp, own_rows + 2, local_width)
        axes, groups_in, stride = ("seq", "tp"), pair * tp, heads_local
    got = lax.all_to_all(sent, axes, 0, 0, tiled=True)
    got = got.reshape(shards, groups_in, own_rows + 2, local_width).astype(f32)
    sums = jnp.sum(got[:, :, :own_rows], axis=0)
    share = got[0, :, own_rows, :] + got[0, :, own_rows + 1, :]
    share = share[:, : own_rows * stride].reshape(groups_in, own_rows, stride)[..., :heads_local]
    share = share / jnp.sum(share, axis=0, keepdims=True)
    sums = sums.reshape(groups_in, own_rows, heads_local, HEAD) * share[..., None]
    return jnp.sum(sums, axis=0).reshape(per, steps, local_width).astype(bf16)


def solution(mesh):
    placed = (
        P("seq", "tp"),
        P("seq", None),
        P(),
        P("seq", None, "tp"),
        P(),
        P(),
        P("seq", "tp"),
        P("seq", "tp"),
        P("seq", "tp"),
    )
    return jax.shard_map(
        on_device, mesh=mesh, in_specs=placed, out_specs=P("seq", None, "tp"), check_vma=False
    )
```

```python
import functools
import math

import jax
import jax.numpy as jnp
from jax import lax
from jax.experimental import pallas as pl
from jax.experimental.pallas import tpu as pltpu
from jax.sharding import PartitionSpec as P

HEAD = 128
PAIR = 2
SLOTS = 4
BLOCKS = 4
NT = (((1,), (1,)), ((), ()))
VMEM_LIMIT = 26 * 1024 * 1024


def params():
    return pltpu.CompilerParams(vmem_limit_bytes=VMEM_LIMIT)


def split(values):
    high = values.astype(jnp.bfloat16)
    return high, (values - high.astype(jnp.float32)).astype(jnp.bfloat16)


def halves(values):
    high = lax.reduce_precision(values, 8, 7)
    return high.astype(jnp.bfloat16), (values - high).astype(jnp.bfloat16)


def thirds(values):
    high = lax.reduce_precision(values, 8, 7)
    return high.astype(jnp.bfloat16), *halves(values - high)


def swap_gather(values, axis, size, index, perm):
    if size == 1:
        return values[None]
    other = lax.ppermute(values, axis, perm)
    first = index == 0
    return jnp.stack([jnp.where(first, values, other), jnp.where(first, other, values)])


def put_lanes(ref, rows, values):
    for tile in range(ref.shape[0]):
        part = values[:, tile * 128 : (tile + 1) * 128]
        if part.shape[1] < 128:
            fill = jnp.zeros((part.shape[0], 128 - part.shape[1]), part.dtype)
            part = jnp.concatenate([part, fill], axis=1)
        ref[tile, rows, :] = part


def take_lanes(ref, rows, width):
    tiles = [ref[tile, rows, :] for tile in range(ref.shape[0])]
    return jnp.concatenate(tiles, axis=1)[:, :width]


def absorb_kernel(count, *refs):
    queries, weights = refs[:count], refs[count : 2 * count]
    gain_ref, out_ref, rows_ref = refs[2 * count :]
    rows, per = queries[0].shape[0], queries[0].shape[1] // HEAD
    gain = gain_ref[...]
    for piece in range(count):
        for head in range(per):
            lanes = pl.ds(head * HEAD, HEAD)
            mixed = lax.dot_general(
                queries[piece][:, lanes], weights[piece][:, lanes], NT,
                preferred_element_type=jnp.float32,
            )
            place = pl.ds(piece * per + head, rows, stride=count * per)
            put_lanes(rows_ref, place, mixed * gain)
    out_ref[...] = take_lanes(rows_ref, slice(None), out_ref.shape[1]).astype(jnp.bfloat16)


def score_tile(slots, per_slot, qk_ref, x, slot):
    tokens = x.shape[0]
    slot = jnp.broadcast_to(slot, (per_slot, tokens))
    depth = SLOTS * per_slot
    scores = jnp.zeros((per_slot, tokens), jnp.float32)
    for group in range(slots // SLOTS):
        part = lax.dot_general(
            qk_ref[group * depth : (group + 1) * depth, :], x, NT,
            preferred_element_type=jnp.float32,
        )
        for j in range(SLOTS):
            here = slot == group * SLOTS + j
            scores = jnp.where(here, part[j * per_slot : (j + 1) * per_slot], scores)
    values = x.astype(jnp.float32)
    high, low = split(values * values)
    ones = jnp.ones((8, x.shape[1]), jnp.bfloat16)
    total = lax.dot_general(ones, high, NT, preferred_element_type=jnp.float32)
    total = total + lax.dot_general(ones, low, NT, preferred_element_type=jnp.float32)
    total_high, total_low = split(total)
    row = lax.broadcasted_iota(jnp.int32, total.shape, 0)
    total = jnp.where(
        row == 0, total_high.astype(jnp.float32), jnp.where(row == 1, total_low.astype(jnp.float32), 0.0)
    )
    return jnp.concatenate([scores, total], axis=0).astype(jnp.bfloat16)


def score_kernel(
    slots, per_slot, new_cols, qk_ref, slot_ref, new_slot_ref, slab_ref, new_ref, out_ref
):
    shards, own, wide = slab_ref.shape
    new = score_tile(slots, per_slot, qk_ref, new_ref[...], new_slot_ref[...])
    batch = BLOCKS if shards % BLOCKS == 0 else 1
    for first in range(0, shards, batch):
        x = slab_ref[first : first + batch].reshape(batch * own, wide)
        slot = slot_ref[:, first * own : (first + batch) * own]
        tile = score_tile(slots, per_slot, qk_ref, x, slot)
        for i in range(batch):
            out_ref[first + i, :, 0:own] = tile[:, i * own : (i + 1) * own]
    for place in range(shards):
        out_ref[place, :, own : own + new_cols] = new[:, place * new_cols : (place + 1) * new_cols]
        rest = out_ref.shape[2] - own - new_cols
        out_ref[place, :, own + new_cols :] = jnp.zeros((per_slot + 8, rest), jnp.bfloat16)


def value_kernel(
    slots, per_slot, new_cols, count, w_ref, slot_ref, gain_ref, slab_ref, new_ref, *refs
):
    weights_in, outs = refs[:count], refs[count : 2 * count]
    d_ref, x_ref, w_all, p_ref, mixed_ref = refs[2 * count :]
    shards, own, _ = slab_ref.shape
    tokens = w_all.shape[1]
    w_all[:, shards * own :] = jnp.zeros((per_slot + 8, tokens - shards * own), jnp.bfloat16)
    for b in range(shards):
        x_ref[b * own : (b + 1) * own, :] = slab_ref[b]
        w_all[:, b * own : (b + 1) * own] = w_ref[b, :, 0:own]
        start = shards * own + b * new_cols
        w_all[:, start : start + new_cols] = w_ref[b, :, own : own + new_cols]
    x_ref[shards * own :, :] = new_ref[...]
    slot = slot_ref[...]
    one_hot = (
        lax.broadcasted_iota(jnp.int32, (slots, tokens), 0) == slot
    ).astype(jnp.float32).astype(jnp.bfloat16)
    weights = w_all[:per_slot, :]
    total = lax.dot_general(weights, one_hot, NT, preferred_element_type=jnp.float32)
    by_slot = lax.dot_general(one_hot, weights, NT, preferred_element_type=jnp.float32)
    steps = d_ref.shape[0] // slots
    heads = per_slot // steps
    fill = jnp.zeros((slots, 128 - heads), jnp.float32)
    for step_id in range(steps):
        part = by_slot[:, step_id * heads : (step_id + 1) * heads]
        d_ref[pl.ds(step_id, slots, stride=steps), :] = jnp.concatenate([part, fill], axis=1)
    inverse = jnp.where(total > 0.0, 1.0 / jnp.where(total > 0.0, total, 1.0), 0.0)
    high, low = split(inverse)
    scale = jnp.dot(high, one_hot, preferred_element_type=jnp.float32)
    scale = scale + jnp.dot(low, one_hot, preferred_element_type=jnp.float32)
    extra = w_all[per_slot:, :].astype(jnp.float32)
    factor = extra[0:1] + extra[1:2]
    p_ref[...] = weights.astype(jnp.float32) * scale * factor
    depth = SLOTS * per_slot
    gain = gain_ref[...]

    def step(group, carry):
        p = p_ref[...]
        wide = jnp.broadcast_to(slot, p.shape)
        rows = [jnp.where(wide == group * SLOTS + j, p, 0.0) for j in range(SLOTS)]
        mixed = jnp.dot(
            jnp.concatenate(rows, axis=0).astype(jnp.bfloat16), x_ref[...],
            preferred_element_type=jnp.float32,
        )
        put_lanes(mixed_ref, pl.ds(pl.multiple_of(group * depth, depth), depth), mixed * gain)
        return carry

    lax.fori_loop(0, slots // SLOTS, step, 0, unroll=8)
    rows, per = outs[0].shape[0], outs[0].shape[1] // HEAD
    for piece in range(count):
        for head in range(per):
            place = pl.ds(piece * per + head, rows, stride=count * per)
            mixed = take_lanes(mixed_ref, place, x_ref.shape[1]).astype(jnp.bfloat16)
            lanes = pl.ds(head * HEAD, HEAD)
            outs[piece][:, lanes] = jnp.dot(
                mixed, weights_in[piece][:, lanes], preferred_element_type=jnp.float32
            ).astype(jnp.bfloat16)


def join_kernel(own_rows, part_ref, theirs_ref, d_ref, theirs_d_ref, out_ref):
    rows, width = part_ref.shape
    heads = width // HEAD
    mine, theirs = d_ref[:, :heads], theirs_d_ref[:, heads : 2 * heads]
    joined = mine + theirs
    inverse = jnp.where(joined > 0.0, 1.0 / jnp.where(joined > 0.0, joined, 1.0), 0.0)
    mine, theirs = mine * inverse, theirs * inverse
    joined = jnp.concatenate([joined, jnp.zeros((rows, 128 - heads), jnp.float32)], axis=1)
    high, low = split(joined)
    high, low = high.astype(jnp.float32), low.astype(jnp.float32)
    for head in range(heads):
        lanes = pl.ds(head * HEAD, HEAD)
        value = part_ref[:, lanes].astype(jnp.float32) * mine[:, head : head + 1]
        value = value + theirs_ref[:, lanes].astype(jnp.float32) * theirs[:, head : head + 1]
        for i in range(rows // own_rows):
            if head < own_rows:
                row = slice(i * own_rows + head, i * own_rows + head + 1)
                extra = [high[row], low[row]]
            else:
                extra = [jnp.zeros((2, HEAD), jnp.float32)]
            block = jnp.concatenate([value[i * own_rows : (i + 1) * own_rows]] + extra, axis=0)
            out_ref[i, :, lanes] = block.astype(jnp.bfloat16)


def on_device(
    slab, token_request, request_slot, new_states, cache_gain, query_gain,
    key_weight, value_weight, query_weight,
):
    f32, bf16 = jnp.float32, jnp.bfloat16
    seq, tp = lax.axis_size("seq"), lax.axis_size("tp")
    k, c = lax.axis_index("seq"), lax.axis_index("tp")
    tokens, half = slab.shape
    model = half * tp
    own = tokens // tp
    feat = model // seq
    pair = PAIR if seq % PAIR == 0 else 1
    shards = seq // pair
    wide = feat * pair
    x, m = k % pair, k // pair
    groups = [[pair * i + p for i in range(shards)] for p in range(pair)]
    x_perm = [(i, i ^ 1) for i in range(seq)]
    tp_perm = [(0, 1), (1, 0)]
    local_width = key_weight.shape[1]
    heads_local = local_width // HEAD
    heads = heads_local * tp
    per, steps, _ = new_states.shape
    slots = request_slot.shape[0]
    own_rows = per * steps
    rows = slots * steps
    per_slot = steps * heads
    scale = 1.0 / math.sqrt(HEAD)

    def over_tp(values):
        if tp == 2:
            return [values, lax.ppermute(values, "tp", tp_perm)]
        everyone = lax.all_gather(values, "tp", axis=0, tiled=False)
        return [everyone[i] for i in range(tp)]

    cut = slab.reshape(tp, own, half)
    if tp == 2:
        mine = lax.dynamic_index_in_dim(cut, c, 0, keepdims=False)
        other = lax.ppermute(
            lax.dynamic_index_in_dim(cut, 1 - c, 0, keepdims=False), "tp", tp_perm
        )
        whole = jnp.stack([jnp.where(c == 0, mine, other), jnp.where(c == 0, other, mine)])
    else:
        whole = lax.all_to_all(cut, "tp", 0, 0, tiled=True)
    message = whole.reshape(tp, own, shards // tp, wide).transpose(0, 2, 1, 3)
    message = message.reshape(shards, own, wide)

    requests = lax.dynamic_index_in_dim(token_request.reshape(tp, own), c, 0, keepdims=False)
    match = requests[None, :] == jnp.arange(slots, dtype=jnp.int32)[:, None]
    target = jnp.sum(jnp.where(match, request_slot[:, None], 0), axis=0)
    states = over_tp(new_states.reshape(own_rows, half))
    if tp == 2:
        states = [jnp.where(c == 0, states[i], states[1 - i]) for i in range(2)]
    states = jnp.concatenate(states, axis=1)
    squares = states.astype(f32)
    own_factor = lax.rsqrt(jnp.mean(squares * squares, axis=-1, keepdims=True) + 1e-06)
    carried = jnp.concatenate([target.astype(bf16), *thirds(own_factor[:, 0])])
    carried_rows = -(-carried.shape[0] // feat)
    carried = jnp.pad(carried, (0, carried_rows * feat - carried.shape[0]))
    carried = jnp.broadcast_to(carried.reshape(1, carried_rows, feat), (seq, carried_rows, feat))
    sent = jnp.concatenate(
        [states.reshape(own_rows, seq, feat).transpose(1, 0, 2), carried], axis=1
    )
    got = lax.all_to_all(sent, "seq", 0, 0, tiled=True)
    state_part = got[:, :own_rows].reshape(rows, feat)
    carried = got[:, own_rows:].reshape(seq, carried_rows * feat)
    slots_in = carried[:, :own].reshape(shards, pair, own)
    slots_in = lax.dynamic_index_in_dim(slots_in, x, 1, keepdims=False).astype(jnp.int32)
    row_factor = carried[:, own : own + 3 * own_rows].astype(f32).reshape(seq, 3, own_rows)
    row_factor = (row_factor[:, 0] + row_factor[:, 1] + row_factor[:, 2]).reshape(rows, 1)

    exchange = functools.partial(
        lax.all_to_all, axis_name="seq", split_axis=0, concat_axis=0, tiled=True,
        axis_index_groups=groups,
    )
    gain_part = lax.dynamic_slice(query_gain, (k * feat,), (feat,))
    query_part = (state_part.astype(f32) * row_factor * gain_part).astype(bf16)
    partial = jnp.dot(query_part, query_weight, preferred_element_type=f32)
    partial = partial.reshape(seq, own_rows, local_width)
    partial = partial.astype(bf16)
    partial = lax.all_to_all(partial, "seq", 0, 0, tiled=True)
    query = jnp.sum(partial.astype(f32), axis=0).astype(bf16)
    queries = exchange(jnp.broadcast_to(query[None], (shards, own_rows, local_width)))
    state_wide = swap_gather(state_part, "seq", pair, x, x_perm)
    queries, state_wide, message, key_weight, value_weight = lax.optimization_barrier(
        (queries, state_wide, message, key_weight, value_weight)
    )
    slab_in = exchange(message)
    queries = swap_gather(queries, "seq", pair, x, x_perm)
    queries = queries.transpose(1, 0, 2, 3).reshape(rows, local_width)
    queries = over_tp(queries)

    def join_pair(first, second):
        if pair == 1:
            return first
        low = x == 0
        return jnp.concatenate(
            [jnp.where(low, first, second), jnp.where(low, second, first)], axis=0
        )

    def from_pair(values):
        return values if pair == 1 else lax.ppermute(values, "seq", x_perm)

    keys_full = over_tp(join_pair(key_weight, from_pair(key_weight)))
    value_other = from_pair(value_weight)
    gain = lax.dynamic_slice(cache_gain, (m * wide,), (wide,)).reshape(1, wide)
    absorbed = pl.pallas_call(
        functools.partial(absorb_kernel, tp),
        out_shape=jax.ShapeDtypeStruct((rows * heads, wide), bf16),
        scratch_shapes=[pltpu.VMEM((-(-wide // 128), rows * heads, 128), f32)],
        compiler_params=params(),
        cost_estimate=pl.CostEstimate(
            flops=2 * rows * heads * HEAD * wide,
            bytes_accessed=2 * (wide + rows) * heads * HEAD,
            transcendentals=0,
        ),
        name="absorb",
    )(*queries, *keys_full, gain)

    new_cols = rows // shards
    width = -(-(own + new_cols) // 128) * 128
    new_width = -(-rows // 128) * 128
    state_wide = state_wide.transpose(1, 0, 2).reshape(rows, wide)
    state_wide = jnp.pad(state_wide, ((0, new_width - rows), (0, 0)))
    group = x * tp + c
    new_slot = jnp.arange(rows, dtype=jnp.int32) // steps
    new_slot = jnp.where(new_slot % (pair * tp) == group, new_slot, -1)
    slot_row = slots_in.reshape(1, shards * own)
    new_row = jnp.pad(new_slot, (0, new_width - rows), constant_values=-1)[None]
    out_rows = per_slot + 8
    partial = pl.pallas_call(
        functools.partial(score_kernel, slots, per_slot, new_cols),
        out_shape=jax.ShapeDtypeStruct((shards, out_rows, width), bf16),
        compiler_params=params(),
        name="scores",
    )(absorbed, slot_row, new_row, slab_in, state_wide)
    partial, value_other = lax.optimization_barrier((partial, value_other))
    partial = lax.all_to_all(partial, "seq", 0, 0, tiled=True, axis_index_groups=groups)
    values_full = [
        join_pair(*blocks) for blocks in zip(over_tp(value_weight), over_tp(value_other))
    ]
    summed = jnp.sum(partial.astype(f32), axis=0)
    mean = (summed[per_slot] + summed[per_slot + 1]) / model
    factor = lax.rsqrt(mean + 1e-06)[None]
    my_new = lax.dynamic_slice(new_slot, (m * new_cols,), (new_cols,))
    spare = jnp.full((width - own - new_cols,), -1, jnp.int32)
    my_slot = jnp.concatenate([target, my_new, spare])[None]
    column = jnp.arange(width, dtype=jnp.int32)[None]
    step_of = jnp.arange(per_slot, dtype=jnp.int32)[:, None] // heads
    seen = (my_slot >= 0) & ((column < own) | ((column - own) % steps <= step_of))
    weights = jnp.where(seen, jnp.exp(summed[:per_slot] * (factor * scale)), 0.0)
    high, low = halves(factor)
    ready = jnp.concatenate(
        [weights.astype(bf16), high, low, jnp.zeros((6, width), bf16)], axis=0
    )
    weights_in = lax.all_to_all(
        jnp.broadcast_to(ready[None], (shards, out_rows, width)),
        "seq", 0, 0, tiled=True, axis_index_groups=groups,
    )

    tokens_all = shards * own + new_width
    *attended, totals = pl.pallas_call(
        functools.partial(value_kernel, slots, per_slot, new_cols, tp),
        out_shape=tuple(
            jax.ShapeDtypeStruct((rows, local_width), bf16) for _ in range(tp)
        ) + (jax.ShapeDtypeStruct((rows, 128), f32),),
        scratch_shapes=[
            pltpu.VMEM((tokens_all, wide), bf16),
            pltpu.VMEM((out_rows, tokens_all), bf16),
            pltpu.VMEM((per_slot, tokens_all), f32),
            pltpu.VMEM((-(-wide // 128), rows * heads, 128), f32),
        ],
        compiler_params=params(),
        name="values",
    )(
        weights_in, jnp.concatenate([slot_row, new_row], axis=1), gain, slab_in, state_wide,
        *values_full,
    )

    if tp == 2 and own_rows <= heads_local:
        sent = pl.pallas_call(
            functools.partial(join_kernel, own_rows),
            out_shape=jax.ShapeDtypeStruct((seq, own_rows + 2, local_width), bf16),
            compiler_params=params(),
            name="join",
        )(
            attended[0], lax.ppermute(attended[1], "tp", tp_perm),
            totals, lax.ppermute(totals, "tp", tp_perm),
        )
        axes, groups_in, stride = "seq", pair, HEAD
    else:
        parts = jnp.stack([part.reshape(seq, own_rows, local_width) for part in attended], axis=1)
        totals = totals[:, :heads].reshape(seq, own_rows, tp, heads_local).transpose(0, 2, 1, 3)
        totals = jnp.stack(halves(totals), axis=2).reshape(seq, tp, 2, own_rows * heads_local)
        spare = local_width - own_rows * heads_local
        totals = jnp.pad(totals, ((0, 0), (0, 0), (0, 0), (0, spare)))
        sent = jnp.concatenate([parts, totals], axis=2)
        sent = sent.reshape(seq * tp, own_rows + 2, local_width)
        axes, groups_in, stride = ("seq", "tp"), pair * tp, heads_local
    got = lax.all_to_all(sent, axes, 0, 0, tiled=True)
    got = got.reshape(shards, groups_in, own_rows + 2, local_width).astype(f32)
    sums = jnp.sum(got[:, :, :own_rows], axis=0)
    share = got[0, :, own_rows, :] + got[0, :, own_rows + 1, :]
    share = share[:, : own_rows * stride].reshape(groups_in, own_rows, stride)[..., :heads_local]
    share = share / jnp.sum(share, axis=0, keepdims=True)
    sums = sums.reshape(groups_in, own_rows, heads_local, HEAD) * share[..., None]
    return jnp.sum(sums, axis=0).reshape(per, steps, local_width).astype(bf16)


def solution(mesh):
    placed = (
        P("seq", "tp"),
        P("seq", None),
        P(),
        P("seq", None, "tp"),
        P(),
        P(),
        P("seq", "tp"),
        P("seq", "tp"),
        P("seq", "tp"),
    )
    return jax.shard_map(
        on_device, mesh=mesh, in_specs=placed, out_specs=P("seq", None, "tp"), check_vma=False
    )
```
